32 devices in a mesh: groups: 2 (over y), gx: 8 (over z, x), gy: 2 (over core).
Axes of the slice: x: 2, y: 2, z: 4, core: 2. Of those that a mesh axis runs over, the one named last changes fastest.
Arguments:
- tokens: bfloat16 [512, 6144], P('groups', ('gy', 'gx')), parts along dimension 0, may hold values from -6 to 6
- ln_gain: bfloat16 [6144], P('gy'), may hold values from 0.099609375 to 1.8984375
- up_weight: bfloat16 [6144, 24576], P('gy', 'gx'), may hold values from -0.078125 to 0.078125
- up_bias: bfloat16 [24576], P('gx'), may hold values from -4 to 4
- down_weight: bfloat16 [24576, 6144], P('gx', 'gy'), may hold values from -0.0546875 to 0.0546875
- down_bias: bfloat16 [6144], P(('gy', 'gx')), may hold values from -3 to 3
Outputs:
- layer_out: bfloat16 [512, 6144], P('groups', ('gy', 'gx')), parts along dimension 0
The draws below stay inside these ranges and needn't reach their ends.
There are 2 independent parts, one for each index of `groups`. The reference program is written for one: setup_inputs(seed, part) draws one part's arguments, and reference() takes and returns one part's arrays. A program takes and returns all parts, laid end to end along the dimension named above; an argument that names none is the same for every part. Nothing has to cross between parts.
All inputs are finite; a program needn't handle non-finite values.
Results may differ from the reference program's by a relative error of at most 0.0049.
Values may be sent and summed in bfloat16 or wider, within the bound.
A program may use at most 128 MiB of HBM per device.

```python
import jax
import jax.numpy as jnp
from jax import lax

D = 6144
FF = 24576
TOKENS = 256


def strengthened(result, rng, source, target, parts, factor):
    def block_of(dim):
        return (jnp.arange(result.shape[dim]) // (result.shape[dim] // parts)).reshape((-1,) + (1,) * (result.ndim - 1 - dim))

    near = jax.random.permutation(rng, parts)[block_of(target)]
    second = (block_of(target) + parts // 2) % parts
    return jnp.where((block_of(source) == near) | (block_of(source) == second), factor * result, result)


def steps_of(own_key, extent, shards, least, high):
    factor_of, own = 1.0, jax.random.fold_in(own_key, 6)
    for axis_at, blocks in shards:
        steps = jnp.exp(jax.random.uniform(jax.random.fold_in(own, axis_at), (blocks,), jnp.float32, least / len(shards), high / len(shards)))
        factor_of = factor_of * jnp.repeat(steps, extent[axis_at] // blocks).reshape([-1 if axis == axis_at else 1 for axis in range(len(extent))])
    return factor_of


def centred(key, dims, deviation, reach, split=(), dtype=jnp.bfloat16):
    gain = steps_of(key, dims, split, -0.22, 0.18) if split else 1.0
    array = jax.random.normal(key, dims, jnp.float32) * deviation * gain
    return jnp.minimum(jnp.maximum(array, -reach), reach).astype(dtype)


def noise_with(stream_key, extent, deviation, reach, split, heavy, kind=jnp.bfloat16):
    array = deviation * jax.random.normal(stream_key, extent, jnp.float32)
    if split:
        array = array * steps_of(stream_key, extent, split, -0.22, 0.18)
    return jnp.clip(strengthened(array, jax.random.fold_in(stream_key, 3), *heavy), -reach, reach).astype(kind)


def setup_inputs(seed: int = 0, part: int = 0) -> dict:
    key_list = jax.random.split(jax.random.key(seed), 7)
    part_splits = jax.random.split(jax.random.fold_in(key_list[6], part), 7)
    return {
        "tokens": centred(part_splits[0], (TOKENS, D), 1.0, 6.0, ((1, 16),)),
        "ln_gain": jnp.clip(1.0 + 0.18 * jax.random.normal(key_list[1], (D,), jnp.float32), 0.099609375, 1.8984375).astype(jnp.bfloat16),
        "up_weight": centred(key_list[2], (D, FF), D ** -0.5, 0.078125, ((0, 2), (1, 8))),
        "up_bias": centred(key_list[3], (FF,), 1.0, 4.0, ((0, 8),)),
        "down_weight": noise_with(key_list[4], (FF, D), FF ** -0.5, 0.0546875, ((0, 8), (1, 2)), (0, 1, 8, 2.0)),
        "down_bias": centred(key_list[5], (D,), 0.5, 3.0, ((0, 16),)),
    }


def reference(tokens, ln_gain, up_weight, up_bias, down_weight, down_bias):
    values = tokens.astype(jnp.float32)
    mean = lax.optimization_barrier(jnp.mean(values, axis=-1, keepdims=True))
    square = lax.optimization_barrier(jnp.mean(values * values, axis=-1, keepdims=True))
    scale = lax.rsqrt(square - mean * mean + 1e-06)
    normed = ((values - mean) * scale * ln_gain.astype(jnp.float32)).astype(jnp.bfloat16)
    pre = jnp.dot(normed, up_weight, preferred_element_type=jnp.float32) + up_bias.astype(jnp.float32)
    hidden = jax.nn.gelu(pre, approximate=False).astype(jnp.bfloat16)
    branch = jnp.dot(hidden, down_weight, preferred_element_type=jnp.float32)
    return (values + branch + down_bias.astype(jnp.float32)).astype(jnp.bfloat16)
```

```python
import functools

import jax
import jax.numpy as jnp
from jax import lax
from jax.experimental import pallas as pl
from jax.experimental.pallas import tpu as pltpu
from jax.sharding import PartitionSpec as P

MESH = pl.DeviceIdType.MESH
F32 = jnp.float32
BF16 = jnp.bfloat16
LINES = 4
CHUNKS = 2
LANES = 128


def normalize(values, first, second, width, gain_part):
    mean = (first / width)[:, None]
    square = (second / width)[:, None]
    scale = lax.rsqrt(square - mean * mean + 1e-06)
    return ((values - mean) * scale * gain_part.astype(jnp.float32)).astype(jnp.bfloat16)


def shards(tokens, ln_gain, up_weight, up_bias, down_weight, down_bias):
    width = tokens.shape[1] * lax.axis_size("gy") * lax.axis_size("gx")
    values = tokens.astype(jnp.float32)
    gathered = lax.all_gather(tokens, "gx", axis=1, tiled=True)
    all_values = gathered.astype(jnp.float32)
    first, second = lax.psum(
        (jnp.sum(all_values, axis=-1), jnp.sum(all_values * all_values, axis=-1)), "gy"
    )
    normed = normalize(all_values, first, second, width, ln_gain)
    partial_value = jnp.dot(normed, up_weight, preferred_element_type=jnp.float32)
    bias_up = up_bias.astype(jnp.float32)
    share = lax.psum_scatter(partial_value, "gy", scatter_dimension=0, tiled=True)
    hidden = jax.nn.gelu(share + bias_up, approximate=False).astype(jnp.bfloat16)
    terms = jnp.dot(
        lax.all_gather(hidden, "gy", axis=0, tiled=True),
        down_weight,
        preferred_element_type=jnp.float32,
    )
    branch = lax.psum_scatter(terms, "gx", scatter_dimension=1, tiled=True)
    return (values + branch + down_bias.astype(jnp.float32)).astype(jnp.bfloat16)


def kernel(
    tok, gain, up_bias, down_bias, wu_hbm, wd_hbm, out,
    wu, wd, line, cross, stat, mean_s, scale_s, nrm, acc, p_out, p_in, h_own, h_other,
    y, x_out, x_in, z_out, z_in,
    wu_sem, wd_sem, st_send, st_recv, az_send, az_recv, ax_send, ax_recv,
    p_sem, h_sem, rx_send, rx_recv, rz_send, rz_recv,
):
    gx, gy = lax.axis_index("gx"), lax.axis_index("gy")
    z, x = gx // 2, gx % 2
    xo, go = 1 - x, 1 - gy
    zs = (z, z + 1 - 2 * (z % 2), (z + 2) % LINES, LINES - 1 - z)
    rows_all, wide = tok.shape
    R = rows_all // CHUNKS
    half = acc.shape[1] // 2
    width = 16 * wide
    to_x = {"gx": z * 2 + xo, "gy": gy}
    to_y = {"gx": gx, "gy": go}
    to_z = [{"gx": zs[j] * 2 + x, "gy": gy} for j in range(LINES)]

    def rows(c):
        return pl.ds(c * R, R)

    def wu_copy(j, a, b):
        src_row = (zs[j] * 2 + (x if a == 0 else xo)) * wide
        src_col = (gy if b == 0 else go) * half
        return pltpu.make_async_copy(
            wu_hbm.at[pl.ds(pl.multiple_of(src_row, wide), wide), pl.ds(pl.multiple_of(src_col, half), half)],
            wu.at[j, pl.ds(a * wide, wide), pl.ds(b * half, half)],
            wu_sem.at[j, a, b],
        )

    def wd_copy(j, a, b):
        src_row = (gy if a == 0 else go) * half
        src_col = (zs[j] * 2 + (x if b == 0 else xo)) * wide
        return pltpu.make_async_copy(
            wd_hbm.at[pl.ds(pl.multiple_of(src_row, half), half), pl.ds(pl.multiple_of(src_col, wide), wide)],
            wd.at[j, pl.ds(a * half, half), pl.ds(b * wide, wide)],
            wd_sem.at[j, a, b],
        )

    four = [(a, b) for a in range(2) for b in range(2)]
    for j in range(LINES):
        for a, b in four:
            wu_copy(j, a, b).start()
    for j in reversed(range(LINES)):
        for a, b in four:
            wd_copy(j, a, b).start()

    me = gx * 2 + gy
    peers = [(me + d) % 16 for d in range(1, 16)]
    barrier = pltpu.get_barrier_semaphore()
    for p in peers:
        pl.semaphore_signal(barrier, inc=1, device_id={"gx": p // 2, "gy": p % 2}, device_id_type=MESH)
    pl.semaphore_wait(barrier, 15)

    def remote(src, dst, send, recv, where):
        return pltpu.make_async_remote_copy(
            src_ref=src, dst_ref=dst, send_sem=send, recv_sem=recv, device_id=where, device_id_type=MESH
        )

    def gather_z(c, j):
        return remote(tok.at[rows(c)], line.at[c, j], az_send.at[c, j], az_recv.at[c, j], to_z[j])

    def gather_x(c, j):
        src = tok.at[rows(c)] if j == 0 else line.at[c, j]
        return remote(src, cross.at[c, j], ax_send.at[c, j], ax_recv.at[c, j], to_x)

    def pre_copy(c):
        return remote(p_out.at[c], p_in.at[c], p_sem.at[c, 0], p_sem.at[c, 1], to_y)

    def hid_copy(c):
        return remote(h_own.at[c], h_other.at[c], h_sem.at[c, 0], h_sem.at[c, 1], to_y)

    def red_x(c, j):
        return remote(x_out.at[c, j], x_in.at[c, j], rx_send.at[c, j], rx_recv.at[c, j], to_x)

    def red_z(c, j):
        return remote(z_out.at[c, j], z_in.at[c, j], rz_send.at[c, j], rz_recv.at[c, j], to_z[j])

    def stat_copy(p):
        return remote(stat.at[me], stat.at[me], st_send.at[p], st_recv.at[me], {"gx": p // 2, "gy": p % 2})

    def stat_arrival(p):
        return remote(stat.at[p], stat.at[p], st_send.at[p], st_recv.at[p], {"gx": p // 2, "gy": p % 2})

    gather_x(0, 0).start()
    for j in range(1, LINES):
        gather_z(0, j).start()

    v = tok[...].astype(F32)
    first = jnp.sum(v, axis=1, keepdims=True)
    second = jnp.sum(v * v, axis=1, keepdims=True)
    lane = lax.broadcasted_iota(jnp.int32, (rows_all, LANES), 1)
    both = jnp.where(lane == 0, first, jnp.where(lane == 1, second, 0.0))
    stat[me] = both.T[0:8, :]
    for p in peers:
        stat_copy(p).start()
    for p in peers:
        stat_arrival(p).wait_recv()
    total = stat[0]
    for i in range(1, 16):
        total = total + stat[i]
    full = jnp.concatenate([total, jnp.zeros((LANES - 8, rows_all), F32)], axis=0).T
    mean = full[:, 0:1] / width
    square = full[:, 1:2] / width
    scale = lax.rsqrt(square - mean * mean + 1e-06)
    mean_s[...] = jnp.broadcast_to(mean, (rows_all, LANES))
    scale_s[...] = jnp.broadcast_to(scale, (rows_all, LANES))

    def norm_into(c, j, a, src):
        col = pl.multiple_of((zs[j] * 2 + (x if a == 0 else xo)) * wide, wide)
        g = gain[:, pl.ds(col, wide)].astype(F32)
        m = jnp.concatenate([mean_s[rows(c), :]] * (wide // LANES), axis=1)
        s = jnp.concatenate([scale_s[rows(c), :]] * (wide // LANES), axis=1)
        nrm[:, a * wide:(a + 1) * wide] = ((src.astype(F32) - m) * s * g).astype(BF16)

    tile = 2 * wide
    tiles = half // tile

    def forward(c, j):
        gather_z(c, j).wait_recv()
        gather_x(c, j).start()

    def up_step(c, j):
        gather_x(c, j).wait_recv()
        norm_into(c, j, 0, tok[rows(c), :] if j == 0 else line[c, j])
        norm_into(c, j, 1, cross[c, j])
        if c == 0:
            for a, b in four:
                wu_copy(j, a, b).wait()

        def body(t, last):
            cols = pl.ds(pl.multiple_of(t * tile, tile), tile)
            part = jnp.dot(nrm[...], wu[j, :, cols], preferred_element_type=F32)
            if j > 0:
                part = part + acc[:, cols]
            if last:
                out_cols = pl.ds(pl.multiple_of((t - tiles) * tile, tile), tile)
                p_out[c, :, out_cols] = part.astype(BF16)
            else:
                acc[:, cols] = part

        if j == LINES - 1:
            pl.loop(tiles, 2 * tiles)(lambda t: body(t, True))
            pre_copy(c).start()
            pl.loop(0, tiles)(lambda t: body(t, False))
        else:
            pl.loop(0, 2 * tiles)(lambda t: body(t, False))

    def activate(c):
        pre_copy(c).wait_recv()
        step = 4 * LANES

        @pl.loop(0, half // step)
        def _(t):
            cols = pl.ds(pl.multiple_of(t * step, step), step)
            bias_cols = pl.ds(pl.multiple_of(gy * half + t * step, step), step)
            pre = acc[:, cols] + p_in[c, :, cols].astype(F32) + up_bias[:, bias_cols].astype(F32)
            h_own[c, :, cols] = (0.5 * pre * (1.0 + lax.erf(pre * 0.7071067811865476))).astype(BF16)

        hid_copy(c).start()

    def down_step(c, j):
        if c == 0:
            for a, b in four:
                wd_copy(j, a, b).wait()
        part = jnp.dot(h_own[c], wd[j, 0:half, :], preferred_element_type=F32)
        part = part + jnp.dot(h_other[c], wd[j, half:, :], preferred_element_type=F32)
        x_out[c, j] = part[:, wide:].astype(BF16)
        red_x(c, j).start()
        y[c, j] = part[:, :wide]

    def pair_step(c, j):
        red_x(c, j).wait_recv()
        both = y[c, j] + x_in[c, j].astype(F32)
        if j == 0:
            y[c, j] = both
        else:
            z_out[c, j] = both.astype(BF16)
            red_z(c, j).start()

    def finish(c):
        res = y[c, 0]
        for j in range(1, LINES):
            red_z(c, j).wait_recv()
            res = res + z_in[c, j].astype(F32)
        res = tok[rows(c), :].astype(F32) + res + down_bias[...].astype(F32)
        out[rows(c), :] = res.astype(BF16)

    forward(0, 1)
    up_step(0, 0)
    forward(0, 2)
    up_step(0, 1)
    forward(0, 3)
    gather_x(1, 0).start()
    for j in range(1, LINES):
        gather_z(1, j).start()
    up_step(0, 2)
    up_step(0, 3)
    forward(1, 1)
    activate(0)
    forward(1, 2)
    up_step(1, 0)
    hid_copy(0).wait_recv()
    down_step(0, 3)
    forward(1, 3)
    down_step(0, 2)
    up_step(1, 1)
    down_step(0, 1)
    down_step(0, 0)
    up_step(1, 2)
    pair_step(0, 3)
    up_step(1, 3)
    pair_step(0, 2)
    activate(1)
    pair_step(0, 1)
    pair_step(0, 0)
    hid_copy(1).wait_recv()
    for j in reversed(range(LINES)):
        down_step(1, j)
    finish(0)
    for j in reversed(range(LINES)):
        pair_step(1, j)
    finish(1)

    for p in peers:
        stat_copy(p).wait_send()
    for c in range(CHUNKS):
        pre_copy(c).wait_send()
        hid_copy(c).wait_send()
        for j in range(LINES):
            gather_x(c, j).wait_send()
            red_x(c, j).wait_send()
            if j > 0:
                gather_z(c, j).wait_send()
                red_z(c, j).wait_send()


def fused(tokens, ln_gain, up_weight, up_bias, down_weight, down_bias):
    T, wide = tokens.shape
    depth, hid = up_weight.shape
    R, half = T // CHUNKS, hid // 2
    vm = pl.BlockSpec(memory_space=pltpu.VMEM)
    hbm = pl.BlockSpec(memory_space=pl.ANY)
    dma = pltpu.SemaphoreType.DMA
    scratch = [
        pltpu.VMEM((LINES, 2 * wide, hid), BF16),
        pltpu.VMEM((LINES, hid, 2 * wide), BF16),
        pltpu.VMEM((CHUNKS, LINES, R, wide), BF16),
        pltpu.VMEM((CHUNKS, LINES, R, wide), BF16),
        pltpu.VMEM((16, 8, T), F32),
        pltpu.VMEM((T, LANES), F32),
        pltpu.VMEM((T, LANES), F32),
        pltpu.VMEM((R, 2 * wide), BF16),
        pltpu.VMEM((R, hid), F32),
        pltpu.VMEM((CHUNKS, R, half), BF16),
        pltpu.VMEM((CHUNKS, R, half), BF16),
        pltpu.VMEM((CHUNKS, R, half), BF16),
        pltpu.VMEM((CHUNKS, R, half), BF16),
        pltpu.VMEM((CHUNKS, LINES, R, wide), F32),
        pltpu.VMEM((CHUNKS, LINES, R, wide), BF16),
        pltpu.VMEM((CHUNKS, LINES, R, wide), BF16),
        pltpu.VMEM((CHUNKS, LINES, R, wide), BF16),
        pltpu.VMEM((CHUNKS, LINES, R, wide), BF16),
        dma((LINES, 2, 2)),
        dma((LINES, 2, 2)),
        dma((16,)),
        dma((16,)),
        dma((CHUNKS, LINES)),
        dma((CHUNKS, LINES)),
        dma((CHUNKS, LINES)),
        dma((CHUNKS, LINES)),
        dma((CHUNKS, 2)),
        dma((CHUNKS, 2)),
        dma((CHUNKS, LINES)),
        dma((CHUNKS, LINES)),
        dma((CHUNKS, LINES)),
        dma((CHUNKS, LINES)),
    ]
    return pl.pallas_call(
        kernel,
        out_shape=jax.ShapeDtypeStruct((T, wide), BF16),
        in_specs=[vm, vm, vm, vm, hbm, hbm],
        out_specs=vm,
        scratch_shapes=scratch,
        compiler_params=pltpu.CompilerParams(
            collective_id=0, has_side_effects=True, vmem_limit_bytes=60 * 1024 * 1024
        ),
        cost_estimate=pl.CostEstimate(
            flops=4 * T * depth * hid, bytes_accessed=4 * depth * hid, transcendentals=T * half
        ),
    )(tokens, ln_gain.reshape(1, -1), up_bias.reshape(1, -1), down_bias.reshape(1, -1), up_weight, down_weight)


def solution(mesh):
    in_specs = (
        P("groups", ("gy", "gx")),
        P("gy"),
        P("gy", "gx"),
        P("gx"),
        P("gx", "gy"),
        P(("gy", "gx")),
    )
    out_specs = P("groups", ("gy", "gx"))
    body = fused if mesh.shape["gx"] == 2 * LINES and mesh.shape["gy"] == 2 else shards
    return jax.shard_map(body, mesh=mesh, in_specs=in_specs, out_specs=out_specs, check_vma=False)
```

```python
import functools

import jax
import jax.numpy as jnp
from jax import lax
from jax.experimental import pallas as pl
from jax.experimental.pallas import tpu as pltpu
from jax.sharding import PartitionSpec as P

MESH = pl.DeviceIdType.MESH
F32 = jnp.float32
BF16 = jnp.bfloat16
LINES = 4
CHUNKS = 2
LANES = 128


def normalize(values, first, second, width, gain_part):
    mean = (first / width)[:, None]
    square = (second / width)[:, None]
    scale = lax.rsqrt(square - mean * mean + 1e-06)
    return ((values - mean) * scale * gain_part.astype(jnp.float32)).astype(jnp.bfloat16)


def shards(tokens, ln_gain, up_weight, up_bias, down_weight, down_bias):
    width = tokens.shape[1] * lax.axis_size("gy") * lax.axis_size("gx")
    values = tokens.astype(jnp.float32)
    gathered = lax.all_gather(tokens, "gx", axis=1, tiled=True)
    all_values = gathered.astype(jnp.float32)
    first, second = lax.psum(
        (jnp.sum(all_values, axis=-1), jnp.sum(all_values * all_values, axis=-1)), "gy"
    )
    normed = normalize(all_values, first, second, width, ln_gain)
    partial_value = jnp.dot(normed, up_weight, preferred_element_type=jnp.float32)
    bias_up = up_bias.astype(jnp.float32)
    share = lax.psum_scatter(partial_value, "gy", scatter_dimension=0, tiled=True)
    hidden = jax.nn.gelu(share + bias_up, approximate=False).astype(jnp.bfloat16)
    terms = jnp.dot(
        lax.all_gather(hidden, "gy", axis=0, tiled=True),
        down_weight,
        preferred_element_type=jnp.float32,
    )
    branch = lax.psum_scatter(terms, "gx", scatter_dimension=1, tiled=True)
    return (values + branch + down_bias.astype(jnp.float32)).astype(jnp.bfloat16)


def kernel(
    tok, gain_in, up_bias_in, down_bias_in, wu_hbm, wd_hbm, out, gain, up_bias, down_bias,
    wu, wd, line, cross, stat, mean_s, scale_s, nrm, acc, p_out, p_in, h_own, h_other,
    y, x_out, x_in, z_out, z_in,
    wu_sem, wd_sem, st_send, st_recv, az_send, az_recv, ax_send, ax_recv,
    p_sem, h_sem, rx_send, rx_recv, rz_send, rz_recv,
):
    gx, gy = lax.axis_index("gx"), lax.axis_index("gy")
    z, x = gx // 2, gx % 2
    xo, go = 1 - x, 1 - gy
    zs = (z, z + 1 - 2 * (z % 2), 2 - z // 2, 3 - 3 * (z // 2))
    mid = (z + 1) // 2 % 2
    middle = mid == 1
    rows_all, wide = tok.shape
    R = rows_all // CHUNKS
    half = acc.shape[2] // 2
    width = 16 * wide
    to_x = {"gx": z * 2 + xo, "gy": gy}
    to_y = {"gx": gx, "gy": go}
    to_next = {"gx": zs[1] * 2 + x, "gy": gy}
    to_middle = {"gx": zs[2] * 2 + x, "gy": gy}
    to_either = {"gx": (zs[1] + mid * (zs[2] - zs[1])) * 2 + x, "gy": gy}

    def rows(c):
        return pl.ds(c * R, R)

    def wu_copy(j, a, b):
        src_row = (zs[j] * 2 + (x if a == 0 else xo)) * wide
        src_col = (gy if b == 0 else go) * half
        return pltpu.make_async_copy(
            wu_hbm.at[pl.ds(pl.multiple_of(src_row, wide), wide), pl.ds(pl.multiple_of(src_col, half), half)],
            wu.at[j, pl.ds(a * wide, wide), pl.ds(b * half, half)],
            wu_sem.at[j, a, b],
        )

    def wd_copy(j, a, b):
        src_row = (gy if a == 0 else go) * half
        src_col = (zs[j] * 2 + (x if b == 0 else xo)) * wide
        return pltpu.make_async_copy(
            wd_hbm.at[pl.ds(pl.multiple_of(src_row, half), half), pl.ds(pl.multiple_of(src_col, wide), wide)],
            wd.at[j, pl.ds(a * half, half), pl.ds(b * wide, wide)],
            wd_sem.at[j, a, b],
        )

    four = [(a, b) for a in range(2) for b in range(2)]
    for j in range(LINES):
        for a, b in four:
            wu_copy(j, a, b).start()
    for j in reversed(range(LINES)):
        for a, b in four:
            wd_copy(j, a, b).start()

    gain[...] = gain_in[...].astype(F32).reshape(1, -1)
    up_bias[...] = up_bias_in[...].astype(F32).reshape(1, -1)
    down_bias[...] = down_bias_in[...].astype(F32).reshape(1, -1)

    me = gx * 2 + gy
    peers = [(me + d) % 16 for d in range(1, 16)]
    barrier = pltpu.get_barrier_semaphore()
    for p in peers:
        pl.semaphore_signal(barrier, inc=1, device_id={"gx": p // 2, "gy": p % 2}, device_id_type=MESH)

    v = tok[...].astype(F32)
    first = jnp.sum(v, axis=1, keepdims=True)
    second = jnp.sum(v * v, axis=1, keepdims=True)
    lane = lax.broadcasted_iota(jnp.int32, (rows_all, LANES), 1)
    both = jnp.where(lane == 0, first, jnp.where(lane == 1, second, 0.0))
    stat[me] = both.T[0:8, :]

    def remote(src, dst, send, recv, where):
        return pltpu.make_async_remote_copy(
            src_ref=src, dst_ref=dst, send_sem=send, recv_sem=recv, device_id=where, device_id_type=MESH
        )

    def gather_z(c, k):
        src = tok.at[rows(c)] if k < 2 else line.at[c, k - 1]
        j = (1, 2, 3, 2, 3)[k]
        where = to_middle if k in (1, 2) else to_next
        return remote(src, line.at[c, j], az_send.at[c, k], az_recv.at[c, j], where)

    def line_arrival(c, j):
        return remote(line.at[c, j], line.at[c, j], az_send.at[c, 0], az_recv.at[c, j], to_next)

    def start_z(c):
        gather_z(c, 0).start()

        @pl.when(middle)
        def _():
            gather_z(c, 1).start()

    def gather_x(c, j):
        src = tok.at[rows(c)] if j == 0 else line.at[c, j]
        return remote(src, cross.at[c, j], ax_send.at[c, j], ax_recv.at[c, j], to_x)

    def pre_copy(c):
        return remote(p_out.at[c], p_in.at[c], p_sem.at[c, 0], p_sem.at[c, 1], to_y)

    def hid_copy(c):
        return remote(h_own.at[c], h_other.at[c], h_sem.at[c, 0], h_sem.at[c, 1], to_y)

    def red_x(c, j):
        return remote(x_out.at[c, j], x_in.at[c, j], rx_send.at[c, j], rx_recv.at[c, j], to_x)

    def red_z(c, j):
        slot = 1 + 3 * mid if j == 1 else j + 2 * mid
        return remote(
            z_out.at[c, j], z_in.at[c, slot], rz_send.at[c, j], rz_recv.at[c, slot], to_next if j == 1 else to_either
        )

    def sum_arrival(c, slot):
        return remote(z_in.at[c, slot], z_in.at[c, slot], rz_send.at[c, 1], rz_recv.at[c, slot], to_next)

    def stat_copy(p):
        return remote(stat.at[me], stat.at[me], st_send.at[p], st_recv.at[me], {"gx": p // 2, "gy": p % 2})

    def stat_arrival(p):
        return remote(stat.at[p], stat.at[p], st_send.at[p], st_recv.at[p], {"gx": p // 2, "gy": p % 2})

    def forward(c, j):
        line_arrival(c, j).wait_recv()
        gather_x(c, j).start()

        @pl.when(middle)
        def _():
            gather_z(c, j + 1).start()

    pl.semaphore_wait(barrier, 15)
    start_z(0)
    gather_x(0, 0).start()
    for p in peers:
        stat_copy(p).start()
    forward(0, 1)
    for p in peers:
        stat_arrival(p).wait_recv()
    total = stat[0]
    for i in range(1, 16):
        total = total + stat[i]
    full = jnp.concatenate([total, jnp.zeros((LANES - 8, rows_all), F32)], axis=0).T
    mean = full[:, 0:1] / width
    square = full[:, 1:2] / width
    scale = lax.rsqrt(square - mean * mean + 1e-06)
    mean_s[...] = jnp.broadcast_to(mean, (rows_all, LANES))
    scale_s[...] = jnp.broadcast_to(scale, (rows_all, LANES))

    def norm_into(c, j, a, src):
        col = pl.multiple_of((zs[j] * 2 + (x if a == 0 else xo)) * wide, wide)
        g = gain[:, pl.ds(col, wide)]
        m = jnp.concatenate([mean_s[rows(c), :]] * (wide // LANES), axis=1)
        s = jnp.concatenate([scale_s[rows(c), :]] * (wide // LANES), axis=1)
        nrm[:, a * wide:(a + 1) * wide] = ((src.astype(F32) - m) * s * g).astype(BF16)

    tile = 2 * wide
    tiles = half // tile

    def up_step(c, j):
        gather_x(c, j).wait_recv()
        norm_into(c, j, 0, tok[rows(c), :] if j == 0 else line[c, j])
        norm_into(c, j, 1, cross[c, j])
        if c == 0:
            for a, b in four:
                wu_copy(j, a, b).wait()

        def body(t, last):
            cols = pl.ds(pl.multiple_of(t * tile, tile), tile)
            part = jnp.dot(nrm[...], wu[j, :, cols], preferred_element_type=F32)
            if j > 0:
                part = part + acc[c, :, cols]
            if last:
                out_cols = pl.ds(pl.multiple_of((t - tiles) * tile, tile), tile)
                p_out[c, :, out_cols] = part.astype(BF16)
            else:
                acc[c, :, cols] = part

        if j == LINES - 1:
            pl.loop(tiles, 2 * tiles)(lambda t: body(t, True))
            pre_copy(c).start()
            pl.loop(0, tiles)(lambda t: body(t, False))
        else:
            pl.loop(0, 2 * tiles)(lambda t: body(t, False))

    def activate(c):
        pre_copy(c).wait_recv()
        step = 4 * LANES

        @pl.loop(0, half // step)
        def _(t):
            cols = pl.ds(pl.multiple_of(t * step, step), step)
            bias_cols = pl.ds(pl.multiple_of(gy * half + t * step, step), step)
            pre = acc[c, :, cols] + p_in[c, :, cols].astype(F32) + up_bias[:, bias_cols]
            h_own[c, :, cols] = (0.5 * pre * (1.0 + lax.erf(pre * 0.7071067811865476))).astype(BF16)

        hid_copy(c).start()

    def down_step(c, j):
        if c == 0:
            for a, b in four:
                wd_copy(j, a, b).wait()
        part = jnp.dot(h_own[c], wd[j, 0:half, :], preferred_element_type=F32)
        part = part + jnp.dot(h_other[c], wd[j, half:, :], preferred_element_type=F32)
        x_out[c, j] = part[:, wide:].astype(BF16)
        red_x(c, j).start()
        y[c, j] = part[:, :wide]

    def pair_step(c, j):
        red_x(c, j).wait_recv()
        y[c, j] = y[c, j] + x_in[c, j].astype(F32)
        if j > 0:
            slot = (0, 5, 2, 3)[j]

            @pl.when(middle)
            def _():
                sum_arrival(c, slot).wait_recv()
                y[c, j] = y[c, j] + z_in[c, slot].astype(F32)

            z_out[c, j] = y[c, j].astype(BF16)
            red_z(c, j).start()

    def finish(c):
        @pl.when(middle)
        def _():
            sum_arrival(c, 1).wait_recv()
            y[c, 0] = y[c, 0] + z_in[c, 1].astype(F32)

        sum_arrival(c, 4).wait_recv()
        res = y[c, 0] + z_in[c, 4].astype(F32)
        res = tok[rows(c), :].astype(F32) + res + down_bias[...]
        out[rows(c), :] = res.astype(BF16)

    forward(0, 2)
    start_z(1)
    up_step(0, 0)
    forward(0, 3)
    gather_x(1, 0).start()
    up_step(0, 1)
    forward(1, 1)
    up_step(0, 2)
    forward(1, 2)
    up_step(0, 3)
    forward(1, 3)
    up_step(1, 0)
    activate(0)
    up_step(1, 1)
    hid_copy(0).wait_recv()
    down_step(0, 3)
    up_step(1, 2)
    down_step(0, 2)
    up_step(1, 3)
    down_step(0, 1)
    pair_step(0, 3)
    down_step(0, 0)
    activate(1)
    pair_step(0, 2)
    pair_step(0, 1)
    pair_step(0, 0)
    hid_copy(1).wait_recv()
    down_step(1, 3)
    down_step(1, 2)
    down_step(1, 1)
    pair_step(1, 3)
    down_step(1, 0)
    finish(0)
    pair_step(1, 2)
    pair_step(1, 1)
    pair_step(1, 0)
    finish(1)

    for p in peers:
        stat_copy(p).wait_send()
    for c in range(CHUNKS):
        pre_copy(c).wait_send()
        hid_copy(c).wait_send()
        for j in range(LINES):
            gather_x(c, j).wait_send()
            red_x(c, j).wait_send()
            if j > 0:
                red_z(c, j).wait_send()
        gather_z(c, 0).wait_send()

        @pl.when(middle)
        def _():
            for k in range(1, 5):
                gather_z(c, k).wait_send()


def fused(tokens, ln_gain, up_weight, up_bias, down_weight, down_bias):
    T, wide = tokens.shape
    depth, hid = up_weight.shape
    R, half = T // CHUNKS, hid // 2
    vm = pl.BlockSpec(memory_space=pltpu.VMEM)
    hbm = pl.BlockSpec(memory_space=pl.ANY)
    dma = pltpu.SemaphoreType.DMA
    scratch = [
        pltpu.VMEM((1, depth), F32),
        pltpu.VMEM((1, hid), F32),
        pltpu.VMEM((1, wide), F32),
        pltpu.VMEM((LINES, 2 * wide, hid), BF16),
        pltpu.VMEM((LINES, hid, 2 * wide), BF16),
        pltpu.VMEM((CHUNKS, LINES, R, wide), BF16),
        pltpu.VMEM((CHUNKS, LINES, R, wide), BF16),
        pltpu.VMEM((16, 8, T), F32),
        pltpu.VMEM((T, LANES), F32),
        pltpu.VMEM((T, LANES), F32),
        pltpu.VMEM((R, 2 * wide), BF16),
        pltpu.VMEM((CHUNKS, R, hid), F32),
        pltpu.VMEM((CHUNKS, R, half), BF16),
        pltpu.VMEM((CHUNKS, R, half), BF16),
        pltpu.VMEM((CHUNKS, R, half), BF16),
        pltpu.VMEM((CHUNKS, R, half), BF16),
        pltpu.VMEM((CHUNKS, LINES, R, wide), F32),
        pltpu.VMEM((CHUNKS, LINES, R, wide), BF16),
        pltpu.VMEM((CHUNKS, LINES, R, wide), BF16),
        pltpu.VMEM((CHUNKS, LINES, R, wide), BF16),
        pltpu.VMEM((CHUNKS, 6, R, wide), BF16),
        dma((LINES, 2, 2)),
        dma((LINES, 2, 2)),
        dma((16,)),
        dma((16,)),
        dma((CHUNKS, 5)),
        dma((CHUNKS, LINES)),
        dma((CHUNKS, LINES)),
        dma((CHUNKS, LINES)),
        dma((CHUNKS, 2)),
        dma((CHUNKS, 2)),
        dma((CHUNKS, LINES)),
        dma((CHUNKS, LINES)),
        dma((CHUNKS, LINES)),
        dma((CHUNKS, 6)),
    ]
    return pl.pallas_call(
        kernel,
        out_shape=jax.ShapeDtypeStruct((T, wide), BF16),
        in_specs=[vm, vm, vm, vm, hbm, hbm],
        out_specs=vm,
        scratch_shapes=scratch,
        compiler_params=pltpu.CompilerParams(
            collective_id=0, has_side_effects=True, vmem_limit_bytes=60 * 1024 * 1024
        ),
        cost_estimate=pl.CostEstimate(
            flops=4 * T * depth * hid, bytes_accessed=4 * depth * hid, transcendentals=T * half
        ),
    )(tokens, ln_gain, up_bias, down_bias, up_weight, down_weight)


def solution(mesh):
    in_specs = (
        P("groups", ("gy", "gx")),
        P("gy"),
        P("gy", "gx"),
        P("gx"),
        P("gx", "gy"),
        P(("gy", "gx")),
    )
    out_specs = P("groups", ("gy", "gx"))
    body = fused if mesh.shape["gx"] == 2 * LINES and mesh.shape["gy"] == 2 else shards
    return jax.shard_map(body, mesh=mesh, in_specs=in_specs, out_specs=out_specs, check_vma=False)
```
